32 devices in a mesh: ep: 4 (over y, x), tp: 8 (over z, core).
Axes of the slice: x: 2, y: 2, z: 4, core: 2. Of those that a mesh axis runs over, the one named last changes fastest.
Arguments:
- tokens: bfloat16 [256, 7168], P(('ep', 'tp')), may hold values from -6 to 6
- cotangent: bfloat16 [256, 7168], P(('ep', 'tp')), may hold values from -6 to 6
- routing: int32 [256, 2], P(('ep', 'tp')), may hold values from 0 to 7, all different within a row; in each aligned block of 8 rows (0 to 7, 8 to 15, ...) at most 3 rows name the same one
- route_gates: bfloat16 [256, 2], P(('ep', 'tp')), may hold values from 0.5 to 2.5
- gate_weight: bfloat16 [8, 2048, 7168], P(None, 'tp', 'ep'), may hold values from -0.0625 to 0.0625
- up_weight: bfloat16 [8, 2048, 7168], P(None, 'tp', 'ep'), may hold values from -0.0625 to 0.0625
- down_weight: bfloat16 [8, 2048, 7168], P(None, 'tp', 'ep'), may hold values from -0.125 to 0.125
Outputs:
- token_grad: bfloat16 [256, 7168], P(('ep', 'tp'))
- route_grad: float32 [256, 2], P(('ep', 'tp'))
- gate_grad: bfloat16 [8, 2048, 7168], P(None, 'tp', 'ep')
- up_grad: bfloat16 [8, 2048, 7168], P(None, 'tp', 'ep')
- down_grad: bfloat16 [8, 2048, 7168], P(None, 'tp', 'ep')
The draws below stay inside these ranges and needn't reach their ends.
Inputs may be any that keep to these rules, and one draw needn't show every extreme that they name: `routing`: in the rows of one device a row names 2 different experts, no expert is named more than 3 times, a bound that some block reaches.
All inputs are finite; a program needn't handle non-finite values.
Results may differ from the reference program's by a relative error of at most 0.017.
Values may be sent and summed in bfloat16 or wider, within the bound.
A program may use at most 192 MiB of HBM per device.

```python
import math
import jax
import jax.numpy as jnp
import numpy as np
from jax import lax

D = 7168
H = 2048
E = 8
TOP = 2
TOK_DEV = 8
MOST = 3
HS = 256
TOKENS = 256
N_EP = 4
N_TP = 8


def level_of(stream_key, dims, split, low, top_value):
    gain = 1.0
    for dim, shards_of in split:
        draws = jax.random.uniform(jax.random.fold_in(jax.random.fold_in(stream_key, 6), dim), (shards_of,), jnp.float32, low / len(split), top_value / len(split))
        gain = gain * jnp.repeat(jnp.exp(draws), dims[dim] // shards_of).reshape((-1,) + (1,) * (len(dims) - 1 - dim))
    return gain


def assign_block(key, own, number, rows, number_of, top, limit, lean):
    sequence = jax.random.permutation(key, number_of)
    crowded, common = shares(number_of, rows * top, limit, lean, True), shares(number_of, rows * top, limit, lean, False)
    places = jnp.arange(number_of)

    def named(sizes, offset_by):
        used = int((sizes > 0).sum())
        fixed = max(1, used // 4)
        shifted = fixed + (places - fixed + offset_by * (used - fixed)) % max(1, number_of - fixed)
        return jnp.zeros((number_of,), jnp.int32).at[sequence[jnp.where(places < fixed, places, shifted)]].set(jnp.asarray(sizes, jnp.int32))

    sizes = jnp.where(number % 4 == 0, named(crowded, number // 4), named(common, number - number // 4 - 1))
    mixed = jax.random.permutation(jax.random.fold_in(own, 3), number_of)
    source_of, sink = mixed[0:number_of // 2 * 2:2], mixed[1:number_of // 2 * 2:2]
    slack = jnp.minimum(sizes[source_of] - 1, limit - sizes[sink]) // 2
    slack = jnp.where((source_of == sequence[0]) | (sink == sequence[0]) | (sizes[sink] == 0), 0, jnp.maximum(slack, 0))
    shifted = jax.random.randint(jax.random.fold_in(own, 4), (number_of // 2,), 0, 1 << 20) % (slack + 1)
    sizes = sizes.at[source_of].add(-shifted).at[sink].add(shifted)
    items = jnp.searchsorted(jnp.cumsum(sizes), jnp.arange(rows * top), side="right").astype(jnp.int32)
    grid = items.reshape(top, rows).T
    grid = grid[jax.random.permutation(jax.random.fold_in(own, 1), rows)]
    offset_by = jax.random.randint(jax.random.fold_in(own, 2), (rows, 1), 0, top)
    return jnp.take_along_axis(grid, (jnp.arange(top)[None, :] + offset_by) % top, axis=1)


def shares(count, total, most, slope, full):
    portions = [(1 << 20) // math.isqrt(rank ** slope) + 1 for rank in range(1, count + 1)]
    largest = most if full else min(most, max(-(-total // count), total * portions[0] // sum(portions)))
    least = 1 if total - largest >= count - 1 else 0
    given, surplus = [largest] + [least] * (count - 1), total - largest - least * (count - 1)
    while surplus > 0:
        free = [i for i in range(1, count) if given[i] < largest] or [i for i in range(1, count) if given[i] < most]
        pool, remaining = sum([portions[i] for i in free]), surplus
        for i in free:
            more = min(most - given[i], max(1, remaining * portions[i] // pool), surplus)
            given[i] = given[i] + more
            surplus = surplus - more
    return np.array(given)


def bell_draw(rng, extent, deviation, most, split=(), kind=jnp.bfloat16):
    result = jax.random.normal(rng, extent, jnp.float32) * deviation
    if len(split) > 0:
        result = level_of(rng, extent, split, -0.22, 0.18) * result
    return jnp.clip(result, min=-most, max=most).astype(kind)


def setup_inputs(seed: int = 0) -> dict:
    keys = jax.random.split(jax.random.key(seed), 8)
    tokens = bell_draw(keys[0], (TOKENS, D), 1.0, 6.0, ((0, 32),))
    cotangent = bell_draw(keys[1], (TOKENS, D), 1.0, 6.0, ((0, 32),))
    routing_keys = jax.random.split(jax.random.fold_in(keys[2], 1), TOKENS // TOK_DEV)
    routing_turns = jax.random.permutation(jax.random.fold_in(keys[2], 3), TOKENS // TOK_DEV)
    routing = jax.vmap(lambda own, number: assign_block(jax.random.fold_in(keys[2], 2), own, number, TOK_DEV, E, TOP, MOST, 2))(routing_keys, routing_turns).reshape((TOKENS, TOP))
    route_gates = jnp.clip(0.5 + 2.0 * jax.random.uniform(keys[3], (TOKENS, TOP), jnp.float32) ** level_of(keys[3], (TOKENS, TOP), ((0, 32),), -0.2, 0.2), 0.5, 2.5).astype(jnp.bfloat16)
    gate_weight = bell_draw(keys[4], (E, H, D), D ** -0.5, 0.0625, ((1, 8), (2, 4)))
    up_weight = bell_draw(keys[5], (E, H, D), D ** -0.5, 0.0625, ((1, 8), (2, 4)))
    down_weight = bell_draw(keys[6], (E, H, D), H ** -0.5, 0.125, ((1, 8), (2, 4)))
    return dict(tokens=tokens, cotangent=cotangent, routing=routing, route_gates=route_gates, gate_weight=gate_weight, up_weight=up_weight, down_weight=down_weight)


def slot_tables(routing):
    devices_all = N_EP * N_TP
    entries = TOK_DEV * TOP
    routes_flat = routing.reshape(devices_all, entries)
    expert_iota = jnp.arange(E, dtype=jnp.int32)
    onehot = (routes_flat[:, :, None] == expert_iota[None, None, :]).astype(jnp.int32)
    before = jnp.cumsum(onehot, axis=1) - onehot
    slot_rank = jnp.sum(before * onehot, axis=2)
    device_ids = jnp.arange(devices_all, dtype=jnp.int32)[:, None]
    slot_index = (device_ids * MOST + slot_rank).reshape(-1).astype(jnp.int32)
    expert_ids = routing.reshape(-1).astype(jnp.int32)
    token_ids = (jnp.arange(TOKENS * TOP, dtype=jnp.int32) // TOP).astype(jnp.int32)
    capacity = devices_all * MOST
    table = jnp.full((E, capacity), TOKENS, jnp.int32).at[expert_ids, slot_index].set(token_ids)
    return expert_ids, slot_index, table


def expert_grads(tokens_pad, cotangent_pad, operands):
    table_row, gate_row, gate_mat, up_mat, down_mat = operands
    rows_x = tokens_pad[table_row]
    rows_dy = cotangent_pad[table_row]
    gate = jnp.dot(rows_x, gate_mat.T, preferred_element_type=jnp.float32)
    upper = jnp.dot(rows_x, up_mat.T, preferred_element_type=jnp.float32)
    hidden = (jax.nn.silu(gate) * upper).astype(jnp.bfloat16)
    factor = gate_row[:, None]
    back = factor * jnp.dot(rows_dy, down_mat.T, preferred_element_type=jnp.float32)
    output = jnp.dot(hidden, down_mat, preferred_element_type=jnp.float32)
    route_term = jnp.sum(rows_dy.astype(jnp.float32) * output, axis=1)
    sigma = jax.nn.sigmoid(gate)
    d_gate = (back * upper * sigma * (1.0 + gate * (1.0 - sigma))).astype(jnp.bfloat16)
    d_up = (back * jax.nn.silu(gate)).astype(jnp.bfloat16)

    def shard_term(total, index):
        start = (index * HS).astype(jnp.int32)
        part_gate = lax.dynamic_slice_in_dim(d_gate, start, HS, 1)
        part_up = lax.dynamic_slice_in_dim(d_up, start, HS, 1)
        mat_gate = lax.dynamic_slice_in_dim(gate_mat, start, HS, 0)
        mat_up = lax.dynamic_slice_in_dim(up_mat, start, HS, 0)
        term = jnp.dot(part_gate, mat_gate, preferred_element_type=jnp.float32)
        term = term + jnp.dot(part_up, mat_up, preferred_element_type=jnp.float32)
        rounded = lax.optimization_barrier(term.astype(jnp.bfloat16))
        return total + rounded.astype(jnp.float32), None

    start_total = jnp.zeros((rows_x.shape[0], D), jnp.float32)
    slot_grad, unused = lax.scan(shard_term, start_total, jnp.arange(H // HS, dtype=jnp.int32))
    grad_gate = jnp.dot(d_gate.T, rows_x, preferred_element_type=jnp.float32).astype(jnp.bfloat16)
    grad_up = jnp.dot(d_up.T, rows_x, preferred_element_type=jnp.float32).astype(jnp.bfloat16)
    scaled = (factor * hidden.astype(jnp.float32)).astype(jnp.bfloat16)
    grad_down = jnp.dot(scaled.T, rows_dy, preferred_element_type=jnp.float32).astype(jnp.bfloat16)
    return slot_grad, route_term, grad_gate, grad_up, grad_down


def partial_expert(tokens_pad, cotangent_pad):
    def apply_one(operands):
        return expert_grads(tokens_pad, cotangent_pad, operands)
    return apply_one


def reference(tokens, cotangent, routing, route_gates, gate_weight, up_weight, down_weight):
    expert_ids, slot_index, table = slot_tables(routing)
    capacity = N_EP * N_TP * MOST
    gate_table = jnp.zeros((E, capacity), jnp.float32).at[expert_ids, slot_index].set(route_gates.reshape(-1).astype(jnp.float32))
    tokens_pad = jnp.concatenate([tokens, jnp.zeros((1, D), tokens.dtype)], axis=0)
    cotangent_pad = jnp.concatenate([cotangent, jnp.zeros((1, D), cotangent.dtype)], axis=0)
    results = lax.map(partial_expert(tokens_pad, cotangent_pad), (table, gate_table, gate_weight, up_weight, down_weight))
    slot_grads, route_terms, gate_grad, up_grad, down_grad = results
    picked = slot_grads[expert_ids, slot_index]
    token_grad = jnp.sum(picked.reshape(TOKENS, TOP, D), axis=1).astype(jnp.bfloat16)
    route_grad = route_terms[expert_ids, slot_index].reshape(TOKENS, TOP)
    return token_grad, route_grad, gate_grad, up_grad, down_grad
```

```python
import jax
import jax.numpy as jnp
from jax import lax
from jax.sharding import PartitionSpec as P


def local(tokens, cotangent, routing, route_gates, gate_weight, up_weight, down_weight):
    rows, width = tokens.shape
    top = routing.shape[1]
    experts, units, part = gate_weight.shape
    ep, tp = lax.axis_size("ep"), lax.axis_size("tp")
    total = ep * tp * rows
    f32, bf16 = jnp.float32, jnp.bfloat16

    both = jnp.stack([tokens, cotangent]).reshape(2 * rows, width)
    both = lax.all_to_all(both, "ep", split_axis=1, concat_axis=0, tiled=True)
    both = lax.all_gather(both, "tp", axis=0, tiled=False).reshape(tp, ep, 2, rows, part)
    x = both[:, :, 0].reshape(total, part)
    dy = both[:, :, 1].reshape(total, part)
    routes = lax.all_gather(lax.all_gather(routing, "ep", axis=0), "tp", axis=0)
    mask = routes.reshape(total, top)[:, :, None] == jnp.arange(experts, dtype=jnp.int32)
    gates = lax.all_gather(route_gates, "tp", axis=0).astype(f32)

    wg = gate_weight.reshape(experts * units, part)
    wu = up_weight.reshape(experts * units, part)
    wd = down_weight.reshape(experts * units, part)

    def pre(a, w):
        full = lax.dot_general(a, w, (((1,), (1,)), ((), ())), preferred_element_type=f32)
        full = full.reshape(total, 1, experts, units)
        return jnp.sum(jnp.where(mask[..., None], full, 0.0), axis=2).astype(bf16)

    partial = jnp.stack([pre(x, wg), pre(x, wu), pre(dy, wd)])
    partial = partial.reshape(3, tp, ep, rows, top, units)
    partial = lax.all_to_all(partial, "ep", split_axis=2, concat_axis=0, tiled=True)
    sums = jnp.sum(partial.reshape(ep, 3, tp, rows, top, units).astype(f32), axis=0)
    gate, upper, reverse = sums[0], sums[1], sums[2]
    factor = gates[..., None]
    sigma = jax.nn.sigmoid(gate)
    silu = gate * sigma
    hidden = (silu * upper).astype(bf16).astype(f32)
    back = factor * reverse
    route_part = jnp.sum(hidden * reverse, axis=-1)
    d_gate = (back * upper * sigma * (1.0 + gate * (1.0 - sigma))).astype(bf16)
    d_up = (back * silu).astype(bf16)
    scaled = (factor * hidden).astype(bf16)
    route_grad = lax.psum_scatter(route_part, "tp", scatter_dimension=0, tiled=False)

    acts = jnp.stack([d_gate, d_up, scaled])
    acts = lax.all_gather(acts, "ep", axis=2).reshape(3, total, top, 1, units)

    def spread(a):
        wide = jnp.where(mask[..., None], a, jnp.zeros((), bf16))
        return jnp.sum(wide, axis=1, dtype=bf16).reshape(total, experts * units)

    dg, du, sc = spread(acts[0]), spread(acts[1]), spread(acts[2])
    dx = jnp.dot(dg, wg, preferred_element_type=f32) + jnp.dot(du, wu, preferred_element_type=f32)
    dx = dx.astype(bf16).reshape(tp, ep, rows, part)
    dx = lax.psum_scatter(dx, "tp", scatter_dimension=0, tiled=False)
    token_grad = lax.all_to_all(dx, "ep", split_axis=0, concat_axis=2, tiled=True).reshape(rows, width)

    def weight(a, b):
        out = lax.dot_general(a, b, (((0,), (0,)), ((), ())), preferred_element_type=f32)
        return out.astype(bf16).reshape(experts, units, part)

    return token_grad, route_grad, weight(dg, x), weight(du, x), weight(sc, dy)


def solution(mesh):
    row, mat = P(("ep", "tp"), None), P(None, "tp", "ep")
    return jax.shard_map(
        local,
        mesh=mesh,
        in_specs=(row, row, row, row, mat, mat, mat),
        out_specs=(row, row, mat, mat, mat),
        check_vma=False,
    )
```

```python
import functools

import jax
import jax.numpy as jnp
from jax import lax
from jax.experimental import pallas as pl
from jax.experimental.pallas import tpu as pltpu
from jax.sharding import PartitionSpec as P

F32, BF16 = jnp.float32, jnp.bfloat16
LANES = 128
VMEM_BYTES = 58 * 1024 * 1024


def main_kernel(
    ep, tp, rows, top,
    src_ref, wg_hbm, wu_hbm, wd_hbm,
    x_ref, y_ref, dg_ref, du_ref, sc_ref, dx_ref, route_ref,
    wg, wu, wd, xy, meta, pick, sel, rcv, acts, acc, rp, rr,
    w_sem, p1_send, p2_send, p3_send, xy_recv, sel_send, sel_recv, act_send, act_recv, rt_send, rt_recv,
):
    me_e, me_t = lax.axis_index("ep"), lax.axis_index("tp")
    experts, units, part = wg.shape
    total = ep * tp * rows
    block = tp * rows
    half = tp // 2
    sibling = me_t + 1 - 2 * lax.rem(me_t, 2)

    def dev(e, t):
        return {"ep": e, "tp": t}

    def remote(src, dst, s_sem, r_sem, e, t):
        return pltpu.make_async_remote_copy(
            src_ref=src, dst_ref=dst, send_sem=s_sem, recv_sem=r_sem,
            device_id=dev(e, t), device_id_type=pl.DeviceIdType.MESH,
        )

    loads = [
        pltpu.make_async_copy(h, v, w_sem.at[i])
        for i, (h, v) in enumerate(((wg_hbm, wg), (wu_hbm, wu), (wd_hbm, wd)))
    ]
    for c in loads:
        c.start()

    barrier = pltpu.get_barrier_semaphore()
    for d in range(1, ep):
        pl.semaphore_signal(
            barrier, inc=1, device_id=dev(lax.rem(me_e + d, ep), me_t), device_id_type=pl.DeviceIdType.MESH
        )
    for d in range(1, tp):
        pl.semaphore_signal(
            barrier, inc=1, device_id=dev(me_e, lax.rem(me_t + d, tp)), device_id_type=pl.DeviceIdType.MESH
        )
    pl.semaphore_wait(barrier, ep - 1 + tp - 1)

    sends = []

    def go(c):
        c.start()
        sends.append(c)

    for d in range(1, ep):
        q = lax.rem(me_e + d, ep)
        go(remote(src_ref.at[q], xy.at[me_e, me_t], p1_send.at[d - 1], xy_recv.at[me_e, me_t], q, me_t))
    xy[me_e, me_t] = src_ref[me_e]

    def landed(s, t):
        remote(xy.at[s, t], xy.at[s, t], p1_send.at[0], xy_recv.at[s, t], me_e, sibling).wait_recv()

    for d in range(ep):
        s = lax.rem(me_e + d, ep)
        if d:
            landed(s, me_t)
        for j in range(half - 1, 0, -1):
            t = lax.rem(me_t + 2 * j, tp)
            go(remote(xy.at[s, me_t], xy.at[s, me_t], p2_send.at[d, j], xy_recv.at[s, me_t], me_e, t))
        go(remote(xy.at[s, me_t], xy.at[s, me_t], p2_send.at[d, 0], xy_recv.at[s, me_t], me_e, sibling))
    for d in range(ep):
        s = lax.rem(me_e + d, ep)
        for j in range(1, half):
            t = lax.rem(me_t + 2 * j, tp)
            landed(s, t)
            go(remote(xy.at[s, t], xy.at[s, t], p3_send.at[d, j - 1], xy_recv.at[s, t], me_e, sibling))
    for d in range(ep):
        s = lax.rem(me_e + d, ep)
        for j in range(half):
            landed(s, lax.rem(sibling + 2 * j, tp))

    def split(s, carry):
        both = xy[s].astype(F32)
        first = pl.multiple_of(s * block, block)
        left = both[:, :rows, :].reshape(block, part + LANES)
        x_ref[pl.ds(first, block), :] = left[:, :part].astype(BF16)
        meta[pl.ds(first, block), :] = left[:, part:]
        y_ref[pl.ds(first, block), :] = both[:, rows:, :part].reshape(block, part).astype(BF16)
        return carry

    lax.fori_loop(0, ep, split, 0)
    for k in range(top):
        pick[k] = jnp.broadcast_to(meta[:, k : k + 1], (total, units))

    for m, (a_ref, w) in enumerate(((x_ref, wg), (x_ref, wu), (y_ref, wd))):
        loads[m].wait()

        def expert(e, carry, a_ref=a_ref, w=w):
            full = lax.dot_general(a_ref[...], w[e], (((1,), (1,)), ((), ())), preferred_element_type=F32)
            here = e.astype(F32)
            for k in range(top):
                acc[k] = jnp.where(pick[k] == here, full, acc[k])
            return carry

        acc[...] = jnp.zeros_like(acc)
        lax.fori_loop(0, experts, expert, 0)
        for k in range(top):
            sel[m, :, k * block : (k + 1) * block, :] = acc[k].astype(BF16).reshape(ep, block, units)
        for d in range(1, ep):
            q = lax.rem(me_e + d, ep)
            go(remote(sel.at[m, q], rcv.at[m, me_e], sel_send.at[m, d - 1], sel_recv.at[m, me_e], q, me_t))

    sums = []
    for m in range(3):
        value = sel[m, me_e].astype(F32)
        for d in range(1, ep):
            s = lax.rem(me_e + d, ep)
            remote(rcv.at[m, s], rcv.at[m, s], p1_send.at[0], sel_recv.at[m, s], s, me_t).wait_recv()
            value = value + rcv[m, s].astype(F32)
        sums.append(value)
    gate, upper, reverse = sums
    mine = meta[pl.ds(pl.multiple_of(me_e * block, block), block), :]
    factor = jnp.concatenate([mine[:, top + k : top + k + 1] for k in range(top)], axis=0)
    sigma = jax.nn.sigmoid(gate)
    silu = gate * sigma
    hidden = (silu * upper).astype(BF16).astype(F32)
    back = factor * reverse
    acts[0, me_e] = (back * upper * sigma * (1.0 + gate * (1.0 - sigma))).astype(BF16)
    acts[1, me_e] = (back * silu).astype(BF16)
    acts[2, me_e] = (factor * hidden).astype(BF16)
    for a in range(3):
        for d in range(1, ep):
            q = lax.rem(me_e + d, ep)
            go(remote(acts.at[a, me_e], acts.at[a, me_e], act_send.at[a, d - 1], act_recv.at[a, me_e], q, me_t))
    term = jnp.sum(hidden * reverse, axis=1, keepdims=True)
    term = jnp.broadcast_to(term, (top * block, LANES))
    for k in range(top):
        rp[:, k] = term[k * block : (k + 1) * block].reshape(tp, rows, LANES)
    for d in range(1, tp):
        t = lax.rem(me_t + d, tp)
        go(remote(rp.at[t], rr.at[me_t], rt_send.at[d - 1], rt_recv.at[me_t], me_e, t))

    for a, out in enumerate((dg_ref, du_ref, sc_ref)):
        for d in range(1, ep):
            s = lax.rem(me_e + d, ep)
            remote(acts.at[a, s], acts.at[a, s], p1_send.at[0], act_recv.at[a, s], s, me_t).wait_recv()
        for k in range(top):
            acc[k] = acts[a, :, k * block : (k + 1) * block, :].reshape(total, units).astype(F32)

        def spread(e, carry, out=out):
            here = e.astype(F32)
            value = jnp.zeros((total, units), F32)
            for k in range(top):
                value = jnp.where(pick[k] == here, acc[k], value)
            out[e] = value.astype(BF16)
            return carry

        lax.fori_loop(0, experts, spread, 0)

    def columns(c, carry):
        at = pl.ds(pl.multiple_of(c * 256, 256), 256)
        value = jnp.zeros((total, 256), F32)
        for e in range(experts):
            value = value + jnp.dot(dg_ref[e], wg[e, :, at], preferred_element_type=F32)
            value = value + jnp.dot(du_ref[e], wu[e, :, at], preferred_element_type=F32)
        dx_ref[:, at] = value.astype(BF16)
        return carry

    lax.fori_loop(0, part // 256, columns, 0)

    value = rp[me_t]
    for d in range(1, tp):
        t = lax.rem(me_t + d, tp)
        remote(rr.at[t], rr.at[t], p1_send.at[0], rt_recv.at[t], me_e, t).wait_recv()
        value = value + rr[t]
    route_ref[...] = value
    for c in sends:
        c.wait_send()


def grad_kernel(dg, du, sc, x, y, gg, ug, wdg):
    for a, b, out in ((dg, x, gg), (du, x, ug), (sc, y, wdg)):
        out[0] = lax.dot_general(
            a[0], b[...], (((0,), (0,)), ((), ())), preferred_element_type=F32
        ).astype(BF16)


def local(tokens, cotangent, routing, route_gates, gate_weight, up_weight, down_weight):
    rows, width = tokens.shape
    top = routing.shape[1]
    experts, units, part = gate_weight.shape
    ep, tp = lax.axis_size("ep"), lax.axis_size("tp")
    total, block, half = ep * tp * rows, tp * rows, tp // 2
    wide = part + LANES

    note = jnp.concatenate([routing.astype(BF16), route_gates], axis=1)
    note = jnp.pad(note, ((0, rows), (0, LANES - 2 * top)))
    both = jnp.concatenate([tokens, cotangent], axis=0).reshape(2 * rows, ep, part).transpose(1, 0, 2)
    src = jnp.concatenate([both, jnp.broadcast_to(note, (ep, 2 * rows, LANES))], axis=2)

    vmem, hbm = pl.BlockSpec(memory_space=pltpu.VMEM), pl.BlockSpec(memory_space=pl.ANY)
    dma = pltpu.SemaphoreType.DMA
    dense = jax.ShapeDtypeStruct((experts, total, units), BF16)
    flat = jax.ShapeDtypeStruct((total, part), BF16)
    x, y, dg, du, sc, dx, route = pl.pallas_call(
        functools.partial(main_kernel, ep, tp, rows, top),
        out_shape=(flat, flat, dense, dense, dense, flat, jax.ShapeDtypeStruct((top, rows, LANES), F32)),
        in_specs=[vmem, hbm, hbm, hbm],
        out_specs=(vmem,) * 7,
        scratch_shapes=[
            pltpu.VMEM((experts, units, part), BF16),
            pltpu.VMEM((experts, units, part), BF16),
            pltpu.VMEM((experts, units, part), BF16),
            pltpu.VMEM((ep, tp, 2 * rows, wide), BF16),
            pltpu.VMEM((total, LANES), F32),
            pltpu.VMEM((top, total, units), F32),
            pltpu.VMEM((3, ep, top * block, units), BF16),
            pltpu.VMEM((3, ep, top * block, units), BF16),
            pltpu.VMEM((3, ep, top * block, units), BF16),
            pltpu.VMEM((top, total, units), F32),
            pltpu.VMEM((tp, top, rows, LANES), F32),
            pltpu.VMEM((tp, top, rows, LANES), F32),
            dma((3,)),
            dma((ep - 1,)),
            dma((ep, half)),
            dma((ep, half)),
            dma((ep, tp)),
            dma((3, ep)),
            dma((3, ep)),
            dma((3, ep)),
            dma((3, ep)),
            dma((tp,)),
            dma((tp,)),
        ],
        compiler_params=pltpu.CompilerParams(
            collective_id=0, has_side_effects=True, vmem_limit_bytes=VMEM_BYTES
        ),
        name="main",
    )(src, gate_weight, up_weight, down_weight)

    dx = lax.psum_scatter(dx.reshape(ep, tp, rows, part), "tp", scatter_dimension=1, tiled=False)

    strip = pl.BlockSpec((1, total, units), lambda e: (e, 0, 0))
    whole = pl.BlockSpec((total, part), lambda e: (0, 0))
    slab = pl.BlockSpec((1, units, part), lambda e: (e, 0, 0))
    grad = jax.ShapeDtypeStruct((experts, units, part), BF16)
    gate_grad, up_grad, down_grad = pl.pallas_call(
        grad_kernel,
        grid=(experts,),
        out_shape=(grad, grad, grad),
        in_specs=[strip, strip, strip, whole, whole],
        out_specs=(slab, slab, slab),
        compiler_params=pltpu.CompilerParams(vmem_limit_bytes=VMEM_BYTES // 2),
        cost_estimate=pl.CostEstimate(
            flops=6 * experts * total * units * part,
            bytes_accessed=6 * experts * units * (part + total) + 4 * total * part,
            transcendentals=0,
        ),
        name="grads",
    )(dg, du, sc, x, y)

    token_grad = lax.all_to_all(dx, "ep", split_axis=0, concat_axis=2, tiled=True).reshape(rows, width)
    return token_grad, route[:, :, 0].T, gate_grad, up_grad, down_grad


def solution(mesh):
    row, mat = P(("ep", "tp"), None), P(None, "tp", "ep")
    return jax.shard_map(
        local,
        mesh=mesh,
        in_specs=(row, row, row, row, mat, mat, mat),
        out_specs=(row, row, mat, mat, mat),
        check_vma=False,
    )
```

```python
import functools

import jax
import jax.numpy as jnp
from jax import lax
from jax.experimental import pallas as pl
from jax.experimental.pallas import tpu as pltpu
from jax.sharding import PartitionSpec as P

F32, BF16 = jnp.float32, jnp.bfloat16
LANES = 128
VMEM_BYTES = 58 * 1024 * 1024


def main_kernel(
    ep, tp, rows, top,
    tok_ref, cot_ref, note_ref, wg_hbm, wu_hbm, wd_hbm,
    x_ref, y_ref, dg_ref, du_ref, sc_ref, grad_ref, route_ref,
    wg, wu, wd, src_ref, xy, meta, pick, sel, rcv, acts, acc, rp, rr,
    w_sem, p1_send, p2_send, p3_send, xy_recv, sel_send, sel_recv, act_send, act_recv, rt_send, rt_recv,
    pieces, sib, pair_sum, got, fin, home, a_send, a_recv, b_send, b_recv, c_send, c_recv,
):
    me_e, me_t = lax.axis_index("ep"), lax.axis_index("tp")
    experts, units, part = wg.shape
    total = ep * tp * rows
    block = tp * rows
    half = tp // 2
    sibling = me_t + 1 - 2 * lax.rem(me_t, 2)

    def dev(e, t):
        return {"ep": e, "tp": t}

    def remote(src, dst, s_sem, r_sem, e, t):
        return pltpu.make_async_remote_copy(
            src_ref=src, dst_ref=dst, send_sem=s_sem, recv_sem=r_sem,
            device_id=dev(e, t), device_id_type=pl.DeviceIdType.MESH,
        )

    loads = [
        pltpu.make_async_copy(h, v, w_sem.at[i])
        for i, (h, v) in enumerate(((wg_hbm, wg), (wu_hbm, wu), (wd_hbm, wd)))
    ]
    for c in loads:
        c.start()

    barrier = pltpu.get_barrier_semaphore()
    for d in range(1, ep):
        pl.semaphore_signal(
            barrier, inc=1, device_id=dev(lax.rem(me_e + d, ep), me_t), device_id_type=pl.DeviceIdType.MESH
        )
    for d in range(1, tp):
        pl.semaphore_signal(
            barrier, inc=1, device_id=dev(me_e, lax.rem(me_t + d, tp)), device_id_type=pl.DeviceIdType.MESH
        )
    note = jnp.concatenate([note_ref[...], jnp.zeros_like(note_ref)], axis=0).astype(BF16)
    for q in range(ep):
        at = slice(q * part, (q + 1) * part)
        both = jnp.concatenate([tok_ref[:, at].astype(F32), cot_ref[:, at].astype(F32)], axis=0)
        src_ref[q, :, :part] = both.astype(BF16)
        src_ref[q, :, part:] = note
    pl.semaphore_wait(barrier, ep - 1 + tp - 1)

    sends = []

    def go(c):
        c.start()
        sends.append(c)

    for d in range(1, ep):
        q = lax.rem(me_e + d, ep)
        go(remote(src_ref.at[q], xy.at[me_e, me_t], p1_send.at[d - 1], xy_recv.at[me_e, me_t], q, me_t))
    xy[me_e, me_t] = src_ref[me_e]

    def landed(s, t):
        remote(xy.at[s, t], xy.at[s, t], p1_send.at[0], xy_recv.at[s, t], me_e, sibling).wait_recv()

    for d in range(ep):
        s = lax.rem(me_e + d, ep)
        if d:
            landed(s, me_t)
        for j in range(half - 1, 0, -1):
            t = lax.rem(me_t + 2 * j, tp)
            go(remote(xy.at[s, me_t], xy.at[s, me_t], p2_send.at[d, j], xy_recv.at[s, me_t], me_e, t))
        go(remote(xy.at[s, me_t], xy.at[s, me_t], p2_send.at[d, 0], xy_recv.at[s, me_t], me_e, sibling))
    for d in range(ep):
        s = lax.rem(me_e + d, ep)
        for j in range(1, half):
            t = lax.rem(me_t + 2 * j, tp)
            landed(s, t)
            go(remote(xy.at[s, t], xy.at[s, t], p3_send.at[d, j - 1], xy_recv.at[s, t], me_e, sibling))
    for d in range(ep):
        s = lax.rem(me_e + d, ep)
        for j in range(half):
            landed(s, lax.rem(sibling + 2 * j, tp))

    def split(s, carry):
        both = xy[s].astype(F32)
        first = pl.multiple_of(s * block, block)
        left = both[:, :rows, :].reshape(block, part + LANES)
        x_ref[pl.ds(first, block), :] = left[:, :part].astype(BF16)
        meta[pl.ds(first, block), :] = left[:, part:]
        y_ref[pl.ds(first, block), :] = both[:, rows:, :part].reshape(block, part).astype(BF16)
        return carry

    lax.fori_loop(0, ep, split, 0)
    for k in range(top):
        pick[k] = jnp.broadcast_to(meta[:, k : k + 1], (total, units))

    for m, (a_ref, w) in enumerate(((x_ref, wg), (x_ref, wu), (y_ref, wd))):
        loads[m].wait()

        def expert(e, carry, a_ref=a_ref, w=w):
            full = lax.dot_general(a_ref[...], w[e], (((1,), (1,)), ((), ())), preferred_element_type=F32)
            here = e.astype(F32)
            for k in range(top):
                acc[k] = jnp.where(pick[k] == here, full, acc[k])
            return carry

        acc[...] = jnp.zeros_like(acc)
        lax.fori_loop(0, experts, expert, 0)
        for k in range(top):
            sel[m, :, k * block : (k + 1) * block, :] = acc[k].astype(BF16).reshape(ep, block, units)
        for d in range(1, ep):
            q = lax.rem(me_e + d, ep)
            go(remote(sel.at[m, q], rcv.at[m, me_e], sel_send.at[m, d - 1], sel_recv.at[m, me_e], q, me_t))

    sums = []
    for m in range(3):
        value = sel[m, me_e].astype(F32)
        for d in range(1, ep):
            s = lax.rem(me_e + d, ep)
            remote(rcv.at[m, s], rcv.at[m, s], p1_send.at[0], sel_recv.at[m, s], s, me_t).wait_recv()
            value = value + rcv[m, s].astype(F32)
        sums.append(value)
    gate, upper, reverse = sums
    mine = meta[pl.ds(pl.multiple_of(me_e * block, block), block), :]
    factor = jnp.concatenate([mine[:, top + k : top + k + 1] for k in range(top)], axis=0)
    sigma = jax.nn.sigmoid(gate)
    silu = gate * sigma
    hidden = (silu * upper).astype(BF16).astype(F32)
    back = factor * reverse
    acts[0, me_e] = (back * upper * sigma * (1.0 + gate * (1.0 - sigma))).astype(BF16)
    acts[1, me_e] = (back * silu).astype(BF16)
    acts[2, me_e] = (factor * hidden).astype(BF16)
    for a in range(3):
        for d in range(1, ep):
            q = lax.rem(me_e + d, ep)
            go(remote(acts.at[a, me_e], acts.at[a, me_e], act_send.at[a, d - 1], act_recv.at[a, me_e], q, me_t))
    term = jnp.sum(hidden * reverse, axis=1, keepdims=True)
    term = jnp.broadcast_to(term, (top * block, LANES))
    for k in range(top):
        rp[:, k] = term[k * block : (k + 1) * block].reshape(tp, rows, LANES)
    for d in range(1, tp):
        t = lax.rem(me_t + d, tp)
        go(remote(rp.at[t], rr.at[me_t], rt_send.at[d - 1], rt_recv.at[me_t], me_e, t))

    def spread_out(a, out):
        for d in range(1, ep):
            s = lax.rem(me_e + d, ep)
            remote(acts.at[a, s], acts.at[a, s], p1_send.at[0], act_recv.at[a, s], s, me_t).wait_recv()
        for k in range(top):
            acc[k] = acts[a, :, k * block : (k + 1) * block, :].reshape(total, units).astype(F32)

        def spread(e, carry):
            here = e.astype(F32)
            value = jnp.zeros((total, units), F32)
            for k in range(top):
                value = jnp.where(pick[k] == here, acc[k], value)
            out[e] = value.astype(BF16)
            return carry

        lax.fori_loop(0, experts, spread, 0)

    spread_out(0, dg_ref)
    spread_out(1, du_ref)

    chunks, span = pieces.shape[0], pieces.shape[-1]
    core = lax.rem(me_t, 2)
    pair = me_t // 2

    def to_core(c):
        return remote(pieces.at[c, 1 - core], sib.at[c], a_send.at[c], a_recv.at[c], me_e, sibling)

    def to_pair(c, j):
        t = lax.rem(me_t + 2 * j, tp)
        return remote(pair_sum.at[c, t // 2], got.at[c, pair], b_send.at[c, j - 1], b_recv.at[c, pair], me_e, t)

    def compute(c):
        at = pl.ds(pl.multiple_of(c * span, span), span)
        value = jnp.zeros((total, span), F32)
        for e in range(experts):
            value = value + jnp.dot(dg_ref[e], wg[e, :, at], preferred_element_type=F32)
            value = value + jnp.dot(du_ref[e], wu[e, :, at], preferred_element_type=F32)
        value = value.reshape(ep, tp, rows, span)
        for t in range(tp):
            pieces[c, t % 2, t // 2] = value[:, t].reshape(ep * rows, span).astype(BF16)
        to_core(c).start()

    def relay(c):
        to_core(c).wait_recv()
        pair_sum[c] = (pieces[c, core].astype(F32) + sib[c].astype(F32)).astype(BF16)
        for j in range(1, half):
            to_pair(c, j).start()

    def step(c, carry):
        compute(c)
        relay(c - 1)
        return carry

    compute(0)
    lax.fori_loop(1, chunks, step, 0)
    relay(chunks - 1)

    spread_out(2, sc_ref)

    def collect(c, carry):
        value = pair_sum[c, pair].astype(F32)
        for j in range(1, half):
            p = lax.rem(pair + j, half)
            remote(got.at[c, p], got.at[c, p], a_send.at[0], b_recv.at[c, p], me_e, sibling).wait_recv()
            value = value + got[c, p].astype(F32)
        at = pl.ds(pl.multiple_of(c * span, span), span)
        fin[:, :, at] = value.reshape(ep, rows, span)
        return carry

    lax.fori_loop(0, chunks, collect, 0)
    for d in range(1, ep):
        q = lax.rem(me_e + d, ep)
        go(remote(fin.at[q], home.at[me_e], c_send.at[d - 1], c_recv.at[me_e], q, me_t))
    home[me_e] = fin[me_e]

    value = rp[me_t]
    for d in range(1, tp):
        t = lax.rem(me_t + d, tp)
        remote(rr.at[t], rr.at[t], p1_send.at[0], rt_recv.at[t], me_e, t).wait_recv()
        value = value + rr[t]
    route_ref[...] = value
    for d in range(1, ep):
        s = lax.rem(me_e + d, ep)
        remote(home.at[s], home.at[s], p1_send.at[0], c_recv.at[s], s, me_t).wait_recv()
    for s in range(ep):
        grad_ref[:, s * part : (s + 1) * part] = home[s].astype(BF16)

    def drain(c, carry):
        to_core(c).wait_send()
        for j in range(1, half):
            to_pair(c, j).wait_send()
        return carry

    lax.fori_loop(0, chunks, drain, 0)
    for c in sends:
        c.wait_send()


def grad_kernel(dg, du, sc, x, y, gg, ug, wdg):
    for a, b, out in ((dg, x, gg), (du, x, ug), (sc, y, wdg)):
        out[0] = lax.dot_general(
            a[0], b[...], (((0,), (0,)), ((), ())), preferred_element_type=F32
        ).astype(BF16)


def local(tokens, cotangent, routing, route_gates, gate_weight, up_weight, down_weight):
    rows, width = tokens.shape
    top = routing.shape[1]
    experts, units, part = gate_weight.shape
    ep, tp = lax.axis_size("ep"), lax.axis_size("tp")
    total, block, half = ep * tp * rows, tp * rows, tp // 2
    wide = part + LANES

    span = 256 if part % 256 == 0 else LANES
    chunks = part // span
    note = jnp.concatenate([routing.astype(F32), route_gates.astype(F32)], axis=1)
    note = jnp.pad(note, ((0, 0), (0, LANES - 2 * top)))

    vmem, hbm = pl.BlockSpec(memory_space=pltpu.VMEM), pl.BlockSpec(memory_space=pl.ANY)
    dma = pltpu.SemaphoreType.DMA
    dense = jax.ShapeDtypeStruct((experts, total, units), BF16)
    flat = jax.ShapeDtypeStruct((total, part), BF16)
    x, y, dg, du, sc, token_grad, route = pl.pallas_call(
        functools.partial(main_kernel, ep, tp, rows, top),
        out_shape=(flat, flat, dense, dense, dense, jax.ShapeDtypeStruct((rows, width), BF16), jax.ShapeDtypeStruct((top, rows, LANES), F32)),
        in_specs=[vmem, vmem, vmem, hbm, hbm, hbm],
        out_specs=(vmem,) * 7,
        scratch_shapes=[
            pltpu.VMEM((experts, units, part), BF16),
            pltpu.VMEM((experts, units, part), BF16),
            pltpu.VMEM((experts, units, part), BF16),
            pltpu.VMEM((ep, 2 * rows, wide), BF16),
            pltpu.VMEM((ep, tp, 2 * rows, wide), BF16),
            pltpu.VMEM((total, LANES), F32),
            pltpu.VMEM((top, total, units), F32),
            pltpu.VMEM((3, ep, top * block, units), BF16),
            pltpu.VMEM((3, ep, top * block, units), BF16),
            pltpu.VMEM((3, ep, top * block, units), BF16),
            pltpu.VMEM((top, total, units), F32),
            pltpu.VMEM((tp, top, rows, LANES), F32),
            pltpu.VMEM((tp, top, rows, LANES), F32),
            dma((3,)),
            dma((ep - 1,)),
            dma((ep, half)),
            dma((ep, half)),
            dma((ep, tp)),
            dma((3, ep)),
            dma((3, ep)),
            dma((3, ep)),
            dma((3, ep)),
            dma((tp,)),
            dma((tp,)),
            pltpu.VMEM((chunks, 2, half, ep * rows, span), BF16),
            pltpu.VMEM((chunks, half, ep * rows, span), BF16),
            pltpu.VMEM((chunks, half, ep * rows, span), BF16),
            pltpu.VMEM((chunks, half, ep * rows, span), BF16),
            pltpu.VMEM((ep, rows, part), F32),
            pltpu.VMEM((ep, rows, part), F32),
            dma((chunks,)),
            dma((chunks,)),
            dma((chunks, half)),
            dma((chunks, half)),
            dma((ep,)),
            dma((ep,)),
        ],
        compiler_params=pltpu.CompilerParams(
            collective_id=0, has_side_effects=True, vmem_limit_bytes=VMEM_BYTES
        ),
        name="main",
    )(tokens, cotangent, note, gate_weight, up_weight, down_weight)

    strip = pl.BlockSpec((1, total, units), lambda e: (e, 0, 0))
    whole = pl.BlockSpec((total, part), lambda e: (0, 0))
    slab = pl.BlockSpec((1, units, part), lambda e: (e, 0, 0))
    grad = jax.ShapeDtypeStruct((experts, units, part), BF16)
    gate_grad, up_grad, down_grad = pl.pallas_call(
        grad_kernel,
        grid=(experts,),
        out_shape=(grad, grad, grad),
        in_specs=[strip, strip, strip, whole, whole],
        out_specs=(slab, slab, slab),
        compiler_params=pltpu.CompilerParams(vmem_limit_bytes=VMEM_BYTES),
        cost_estimate=pl.CostEstimate(
            flops=6 * experts * total * units * part,
            bytes_accessed=6 * experts * units * (part + total) + 4 * total * part,
            transcendentals=0,
        ),
        name="grads",
    )(dg, du, sc, x, y)

    return token_grad, route[:, :, 0].T, gate_grad, up_grad, down_grad


def solution(mesh):
    row, mat = P(("ep", "tp"), None), P(None, "tp", "ep")
    return jax.shard_map(
        local,
        mesh=mesh,
        in_specs=(row, row, row, row, mat, mat, mat),
        out_specs=(row, row, mat, mat, mat),
        check_vma=False,
    )
```

```python
import functools

import jax
import jax.numpy as jnp
from jax import lax
from jax.experimental import pallas as pl
from jax.experimental.pallas import tpu as pltpu
from jax.sharding import PartitionSpec as P

F32, BF16 = jnp.float32, jnp.bfloat16
LANES = 128
VMEM_BYTES = 58 * 1024 * 1024


def main_kernel(
    ep, tp, rows, top,
    tok_ref, cot_ref, note_ref, wg_hbm, wu_hbm, wd_hbm,
    x_ref, y_ref, dg_ref, du_ref, sc_ref, grad_ref, route_ref,
    wg, wu, wd, src_ref, xy, meta, pick, sel, rcv, acts, acc, rp, rr,
    w_sem, p1_send, p2_send, p3_send, xy_recv, sel_send, sel_recv, act_send, act_recv, rt_send, rt_recv,
    pieces, sib, pair_sum, got, fin, home, a_send, a_recv, b_send, b_recv, c_send, c_recv,
):
    me_e, me_t = lax.axis_index("ep"), lax.axis_index("tp")
    experts, units, part = wg.shape
    total = ep * tp * rows
    block = tp * rows
    half = tp // 2
    sibling = me_t + 1 - 2 * lax.rem(me_t, 2)

    def dev(e, t):
        return {"ep": e, "tp": t}

    def remote(src, dst, s_sem, r_sem, e, t):
        return pltpu.make_async_remote_copy(
            src_ref=src, dst_ref=dst, send_sem=s_sem, recv_sem=r_sem,
            device_id=dev(e, t), device_id_type=pl.DeviceIdType.MESH,
        )

    loads = [
        pltpu.make_async_copy(h, v, w_sem.at[i])
        for i, (h, v) in enumerate(((wg_hbm, wg), (wu_hbm, wu), (wd_hbm, wd)))
    ]
    for c in loads:
        c.start()

    barrier = pltpu.get_barrier_semaphore()
    for d in range(1, ep):
        pl.semaphore_signal(
            barrier, inc=1, device_id=dev(lax.rem(me_e + d, ep), me_t), device_id_type=pl.DeviceIdType.MESH
        )
    for d in range(1, tp):
        pl.semaphore_signal(
            barrier, inc=1, device_id=dev(me_e, lax.rem(me_t + d, tp)), device_id_type=pl.DeviceIdType.MESH
        )
    note = jnp.concatenate([note_ref[...], jnp.zeros_like(note_ref)], axis=0).astype(BF16)
    fold = part // 2
    for i, ref in enumerate((tok_ref, cot_ref)):
        for q in range(ep):
            low, mid, high = q * part, q * part + fold, (q + 1) * part
            both = jnp.concatenate([ref[:, low:mid].astype(F32), ref[:, mid:high].astype(F32)], axis=0)
            src_ref[i, q, :, :fold] = both.astype(BF16)
            src_ref[i, q, :, fold:] = note
    pl.semaphore_wait(barrier, ep - 1 + tp - 1)

    sends = []

    def go(c):
        c.start()
        sends.append(c)

    for i in range(2):
        for d in range(1, ep):
            q = lax.rem(me_e + d, ep)
            go(remote(
                src_ref.at[i, q], xy.at[i, me_e, me_t], p1_send.at[i, d - 1], xy_recv.at[i, me_e, me_t], q, me_t
            ))
        xy[i, me_e, me_t] = src_ref[i, me_e]

    def landed(i, s, t):
        here = xy.at[i, s, t]
        remote(here, here, p1_send.at[0, 0], xy_recv.at[i, s, t], me_e, sibling).wait_recv()

    def along(i):
        for d in range(ep):
            s = lax.rem(me_e + d, ep)
            if d:
                landed(i, s, me_t)
            here = xy.at[i, s, me_t]
            for j in range(half - 1, 0, -1):
                t = lax.rem(me_t + 2 * j, tp)
                go(remote(here, here, p2_send.at[i, d, j], xy_recv.at[i, s, me_t], me_e, t))
            go(remote(here, here, p2_send.at[i, d, 0], xy_recv.at[i, s, me_t], me_e, sibling))

    def across(i):
        for d in range(ep):
            s = lax.rem(me_e + d, ep)
            for j in range(1, half):
                t = lax.rem(me_t + 2 * j, tp)
                landed(i, s, t)
                here = xy.at[i, s, t]
                go(remote(here, here, p3_send.at[i, d, j - 1], xy_recv.at[i, s, t], me_e, sibling))

    def unfold(i, out):
        for d in range(ep):
            s = lax.rem(me_e + d, ep)
            for j in range(half):
                landed(i, s, lax.rem(sibling + 2 * j, tp))

        def split(s, carry):
            both = xy[i, s].astype(F32)
            at = pl.ds(pl.multiple_of(s * block, block), block)
            left, right = both[:, :rows, :], both[:, rows:, :fold]
            out[at, :fold] = left[:, :, :fold].reshape(block, fold).astype(BF16)
            out[at, fold:] = right.reshape(block, fold).astype(BF16)
            if i == 0:
                meta[at, :] = left[:, :, fold:].reshape(block, LANES)
            return carry

        lax.fori_loop(0, ep, split, 0)

    along(0)
    along(1)
    across(0)
    unfold(0, x_ref)
    for k in range(top):
        pick[k] = jnp.broadcast_to(meta[:, k : k + 1], (total, units))

    for m, (a_ref, w) in enumerate(((x_ref, wg), (x_ref, wu), (y_ref, wd))):
        loads[m].wait()

        if m == 1:
            across(1)
        if m == 2:
            unfold(1, y_ref)
        for e in range(experts):
            full = lax.dot_general(a_ref[...], w[e], (((1,), (1,)), ((), ())), preferred_element_type=F32)
            for k in range(top):
                acc[k] = jnp.where(pick[k] == float(e), full, acc[k] if e else 0.0)
        for k in range(top):
            sel[m, :, k * block : (k + 1) * block, :] = acc[k].astype(BF16).reshape(ep, block, units)
        for d in range(1, ep):
            q = lax.rem(me_e + d, ep)
            go(remote(sel.at[m, q], rcv.at[m, me_e], sel_send.at[m, d - 1], sel_recv.at[m, me_e], q, me_t))

    sums = []
    for m in range(3):
        value = sel[m, me_e].astype(F32)
        for d in range(1, ep):
            s = lax.rem(me_e + d, ep)
            remote(rcv.at[m, s], rcv.at[m, s], p1_send.at[0, 0], sel_recv.at[m, s], s, me_t).wait_recv()
            value = value + rcv[m, s].astype(F32)
        sums.append(value)
    gate, upper, reverse = sums
    mine = meta[pl.ds(pl.multiple_of(me_e * block, block), block), :]
    factor = jnp.concatenate([mine[:, top + k : top + k + 1] for k in range(top)], axis=0)
    sigma = jax.nn.sigmoid(gate)
    silu = gate * sigma
    hidden = (silu * upper).astype(BF16).astype(F32)
    back = factor * reverse
    acts[0, me_e] = (back * upper * sigma * (1.0 + gate * (1.0 - sigma))).astype(BF16)
    acts[1, me_e] = (back * silu).astype(BF16)
    acts[2, me_e] = (factor * hidden).astype(BF16)
    for a in range(3):
        for d in range(1, ep):
            q = lax.rem(me_e + d, ep)
            go(remote(acts.at[a, me_e], acts.at[a, me_e], act_send.at[a, d - 1], act_recv.at[a, me_e], q, me_t))
    term = jnp.sum(hidden * reverse, axis=1, keepdims=True)
    term = jnp.broadcast_to(term, (top * block, LANES))
    for k in range(top):
        rp[:, k] = term[k * block : (k + 1) * block].reshape(tp, rows, LANES)
    for d in range(1, tp):
        t = lax.rem(me_t + d, tp)
        go(remote(rp.at[t], rr.at[me_t], rt_send.at[d - 1], rt_recv.at[me_t], me_e, t))

    def spread_out(a, out):
        for d in range(1, ep):
            s = lax.rem(me_e + d, ep)
            remote(acts.at[a, s], acts.at[a, s], p1_send.at[0, 0], act_recv.at[a, s], s, me_t).wait_recv()
        for k in range(top):
            acc[k] = acts[a, :, k * block : (k + 1) * block, :].reshape(total, units).astype(F32)

        def spread(e, carry):
            here = e.astype(F32)
            value = jnp.zeros((total, units), F32)
            for k in range(top):
                value = jnp.where(pick[k] == here, acc[k], value)
            out[e] = value.astype(BF16)
            return carry

        lax.fori_loop(0, experts, spread, 0)

    spread_out(0, dg_ref)
    spread_out(1, du_ref)

    chunks, span = pieces.shape[0], pieces.shape[-1]
    core = lax.rem(me_t, 2)
    pair = me_t // 2

    def to_core(c):
        return remote(pieces.at[c, 1 - core], sib.at[c], a_send.at[c], a_recv.at[c], me_e, sibling)

    def to_pair(c, j):
        t = lax.rem(me_t + 2 * j, tp)
        return remote(pair_sum.at[c, t // 2], got.at[c, pair], b_send.at[c, j - 1], b_recv.at[c, pair], me_e, t)

    def compute(c):
        at = pl.ds(pl.multiple_of(c * span, span), span)
        value = jnp.zeros((total, span), F32)
        for e in range(experts):
            value = value + jnp.dot(dg_ref[e], wg[e, :, at], preferred_element_type=F32)
            value = value + jnp.dot(du_ref[e], wu[e, :, at], preferred_element_type=F32)
        value = value.reshape(ep, tp, rows, span)
        for t in range(tp):
            pieces[c, t % 2, t // 2] = value[:, t].reshape(ep * rows, span).astype(BF16)
        to_core(c).start()

    def relay(c):
        to_core(c).wait_recv()
        pair_sum[c] = (pieces[c, core].astype(F32) + sib[c].astype(F32)).astype(BF16)
        for j in range(1, half):
            to_pair(c, j).start()

    def step(c, carry):
        compute(c)
        relay(c - 1)
        return carry

    compute(0)
    lax.fori_loop(1, chunks, step, 0)
    relay(chunks - 1)

    spread_out(2, sc_ref)

    def collect(c, carry):
        value = pair_sum[c, pair].astype(F32)
        for j in range(1, half):
            p = lax.rem(pair + j, half)
            remote(got.at[c, p], got.at[c, p], a_send.at[0], b_recv.at[c, p], me_e, sibling).wait_recv()
            value = value + got[c, p].astype(F32)
        at = pl.ds(pl.multiple_of(c * span, span), span)
        fin[:, :, at] = value.reshape(ep, rows, span)
        return carry

    lax.fori_loop(0, chunks, collect, 0)
    for d in range(1, ep):
        q = lax.rem(me_e + d, ep)
        go(remote(fin.at[q], home.at[me_e], c_send.at[d - 1], c_recv.at[me_e], q, me_t))
    home[me_e] = fin[me_e]

    value = rp[me_t]
    for d in range(1, tp):
        t = lax.rem(me_t + d, tp)
        remote(rr.at[t], rr.at[t], p1_send.at[0, 0], rt_recv.at[t], me_e, t).wait_recv()
        value = value + rr[t]
    for k in range(top):
        route_ref[:, k : k + 1] = value[k, :, :1]
    for d in range(1, ep):
        s = lax.rem(me_e + d, ep)
        remote(home.at[s], home.at[s], p1_send.at[0, 0], c_recv.at[s], s, me_t).wait_recv()
    for s in range(ep):
        grad_ref[:, s * part : (s + 1) * part] = home[s].astype(BF16)

    def drain(c, carry):
        to_core(c).wait_send()
        for j in range(1, half):
            to_pair(c, j).wait_send()
        return carry

    lax.fori_loop(0, chunks, drain, 0)
    for c in sends:
        c.wait_send()


def grad_kernel(dg, du, sc, x, y, gg, ug, wdg):
    for a, b, out in ((dg, x, gg), (du, x, ug), (sc, y, wdg)):
        out[0] = lax.dot_general(
            a[0], b[...], (((0,), (0,)), ((), ())), preferred_element_type=F32
        ).astype(BF16)


def local(tokens, cotangent, routing, route_gates, gate_weight, up_weight, down_weight):
    rows, width = tokens.shape
    top = routing.shape[1]
    experts, units, part = gate_weight.shape
    ep, tp = lax.axis_size("ep"), lax.axis_size("tp")
    total, block, half = ep * tp * rows, tp * rows, tp // 2
    wide = part // 2 + LANES

    span = 256 if part % 256 == 0 else LANES
    chunks = part // span
    note = jnp.concatenate([routing.astype(F32), route_gates.astype(F32)], axis=1)
    note = jnp.pad(note, ((0, 0), (0, LANES - 2 * top)))

    vmem, hbm = pl.BlockSpec(memory_space=pltpu.VMEM), pl.BlockSpec(memory_space=pl.ANY)
    dma = pltpu.SemaphoreType.DMA
    dense = jax.ShapeDtypeStruct((experts, total, units), BF16)
    flat = jax.ShapeDtypeStruct((total, part), BF16)
    x, y, dg, du, sc, token_grad, route = pl.pallas_call(
        functools.partial(main_kernel, ep, tp, rows, top),
        out_shape=(flat, flat, dense, dense, dense, jax.ShapeDtypeStruct((rows, width), BF16), jax.ShapeDtypeStruct((rows, top), F32)),
        in_specs=[vmem, vmem, vmem, hbm, hbm, hbm],
        out_specs=(vmem,) * 7,
        scratch_shapes=[
            pltpu.VMEM((experts, units, part), BF16),
            pltpu.VMEM((experts, units, part), BF16),
            pltpu.VMEM((experts, units, part), BF16),
            pltpu.VMEM((2, ep, 2 * rows, wide), BF16),
            pltpu.VMEM((2, ep, tp, 2 * rows, wide), BF16),
            pltpu.VMEM((total, LANES), F32),
            pltpu.VMEM((top, total, units), F32),
            pltpu.VMEM((3, ep, top * block, units), BF16),
            pltpu.VMEM((3, ep, top * block, units), BF16),
            pltpu.VMEM((3, ep, top * block, units), BF16),
            pltpu.VMEM((top, total, units), F32),
            pltpu.VMEM((tp, top, rows, LANES), F32),
            pltpu.VMEM((tp, top, rows, LANES), F32),
            dma((3,)),
            dma((2, ep - 1)),
            dma((2, ep, half)),
            dma((2, ep, half)),
            dma((2, ep, tp)),
            dma((3, ep)),
            dma((3, ep)),
            dma((3, ep)),
            dma((3, ep)),
            dma((tp,)),
            dma((tp,)),
            pltpu.VMEM((chunks, 2, half, ep * rows, span), BF16),
            pltpu.VMEM((chunks, half, ep * rows, span), BF16),
            pltpu.VMEM((chunks, half, ep * rows, span), BF16),
            pltpu.VMEM((chunks, half, ep * rows, span), BF16),
            pltpu.VMEM((ep, rows, part), F32),
            pltpu.VMEM((ep, rows, part), F32),
            dma((chunks,)),
            dma((chunks,)),
            dma((chunks, half)),
            dma((chunks, half)),
            dma((ep,)),
            dma((ep,)),
        ],
        compiler_params=pltpu.CompilerParams(
            collective_id=0, has_side_effects=True, vmem_limit_bytes=VMEM_BYTES
        ),
        name="main",
    )(tokens, cotangent, note, gate_weight, up_weight, down_weight)

    strip = pl.BlockSpec((1, total, units), lambda e: (e, 0, 0))
    whole = pl.BlockSpec((total, part), lambda e: (0, 0))
    slab = pl.BlockSpec((1, units, part), lambda e: (e, 0, 0))
    grad = jax.ShapeDtypeStruct((experts, units, part), BF16)
    gate_grad, up_grad, down_grad = pl.pallas_call(
        grad_kernel,
        grid=(experts,),
        out_shape=(grad, grad, grad),
        in_specs=[strip, strip, strip, whole, whole],
        out_specs=(slab, slab, slab),
        compiler_params=pltpu.CompilerParams(vmem_limit_bytes=VMEM_BYTES),
        cost_estimate=pl.CostEstimate(
            flops=6 * experts * total * units * part,
            bytes_accessed=6 * experts * units * (part + total) + 4 * total * part,
            transcendentals=0,
        ),
        name="grads",
    )(dg, du, sc, x, y)

    return token_grad, route, gate_grad, up_grad, down_grad


def solution(mesh):
    row, mat = P(("ep", "tp"), None), P(None, "tp", "ep")
    return jax.shard_map(
        local,
        mesh=mesh,
        in_specs=(row, row, row, row, mat, mat, mat),
        out_specs=(row, row, mat, mat, mat),
        check_vma=False,
    )
```
